32 devices in a mesh: scene: 2 (over y), bins: 4 (over z), az: 4 (over x, core).
Axes of the slice: x: 2, y: 2, z: 4, core: 2. Of those that a mesh axis runs over, the one named last changes fastest.
Arguments:
- raw_echoes: bfloat16 [2, 8, 512, 16384], P(None, ('scene', 'az'), 'bins'), parts along dimension 1, may hold values from -6 to 6
- range_phase: float32 [16384], replicated, may hold values from -3.140625 to 3.140625
- band_start: int32 [16384], replicated, may hold values from 0 to 16447, as said below
- band_weight: bfloat16 [8, 16384], replicated, may hold values from -0.25 to 0.75
- intersection_length: int32 [16384], P('bins'), may hold values from 32 to 128
- azimuth_rate: float32 [16384], P('bins'), may hold values from 0.25 to 2
Outputs:
- focused_image: bfloat16 [2, 8, 512, 16384], P(None, ('scene', 'az'), None, 'bins'), parts along dimension 1
The draws below stay inside these ranges and needn't reach their ends.
There are 2 independent parts, one for each index of `scene`. The reference program is written for one: setup_inputs(seed, part) draws one part's arguments, and reference() takes and returns one part's arrays. A program takes and returns all parts, laid end to end along the dimension named above; an argument that names none is the same for every part. Nothing has to cross between parts.
Inputs may be any that keep to these rules, and one draw needn't show every extreme that they name: band_start[b] - b lies between 0 and 64 for every range bin b.
All inputs are finite; a program needn't handle non-finite values.
Results may differ from the reference program's by a relative error of at most 0.02.
Values may be sent and summed in bfloat16 or wider, within the bound.
No kernel may reach another device: no remote copies, remote signals or barrier semaphores. Data moves between devices by JAX's collectives and lax.ppermute only.
A program may use at most 128 MiB of HBM per device.

```python
import math
import jax
import jax.numpy as jnp
from jax import lax

NR = 16384
SUBP = 512
OVLMAX = 128
TAPS = 8
SHIFT = 64
N_AZ = 4


def draw_band_start(key, part):
    first_key = jax.random.fold_in(key, 11)
    offsets = jax.random.randint(first_key, (NR,), 0, SHIFT + 1)
    positions = jnp.arange(NR)
    offsets = jnp.where(positions == NR - 1, SHIFT, offsets)
    offsets = jnp.where(positions == 0, 0, offsets)
    return (positions + offsets).astype(jnp.int32)


def draw_intersection_length(key, part):
    first_key, second_key = jax.random.split(jax.random.fold_in(key, 23))
    lengths = jax.random.randint(first_key, (NR,), OVLMAX // 4, OVLMAX + 1)
    chosen = jax.random.randint(second_key, (), 0, NR)
    lengths = jnp.where(jnp.arange(NR) == chosen, OVLMAX, lengths)
    return lengths.astype(jnp.int32)


def block_scale(rng, shape, shards, low, high):
    level = 1.0
    for axis_at, parts in shards:
        heights = jax.random.uniform(jax.random.fold_in(jax.random.fold_in(rng, 6), axis_at), (parts,), jnp.float32, low / len(shards), high / len(shards))
        level = level * jnp.repeat(jnp.exp(heights), shape[axis_at] // parts).reshape((-1,) + (1,) * (len(shape) - 1 - axis_at))
    return level


def bell_draw(own_key, shape, spread, reach, cuts=(), held_as=jnp.bfloat16):
    gain = block_scale(own_key, shape, cuts, -0.22, 0.18) if cuts else 1.0
    values = jax.random.normal(own_key, shape, jnp.float32) * spread * gain
    return jnp.minimum(jnp.maximum(values, -reach), reach).astype(held_as)


def setup_inputs(seed: int = 0, part: int = 0) -> dict:
    splits = jax.random.split(jax.random.key(seed), 7)
    part_splits = jax.random.split(jax.random.fold_in(splits[6], part), 7)
    raw_echoes = bell_draw(part_splits[0], (2, N_AZ, SUBP, NR), 1.0, 6.0, ((1, 4), (2, 4)))
    range_phase = jnp.clip(jax.random.uniform(splits[1], (NR,), jnp.float32, -3.140625, 3.140625), -3.140625, 3.140625)
    band_start = draw_band_start(jax.random.fold_in(splits[6], 71), part)
    band_weight = jnp.clip(jax.random.uniform(splits[3], (TAPS, NR), jnp.float32, -0.25, 0.75), -0.25, 0.75).astype(jnp.bfloat16)
    intersection_length = draw_intersection_length(jax.random.fold_in(splits[6], 71), part)
    azimuth_rate = jnp.clip(jnp.exp(math.log(2.0) - 2.0794415 * jax.random.uniform(splits[5], (NR,), jnp.float32) ** block_scale(splits[5], (NR,), ((0, 4),), -0.2, 0.2)), 0.25, 2.0)
    return {"raw_echoes": raw_echoes, "range_phase": range_phase, "band_start": band_start, "band_weight": band_weight, "intersection_length": intersection_length, "azimuth_rate": azimuth_rate}


def round_pair(values):
    return jnp.real(values).astype(jnp.bfloat16), jnp.imag(values).astype(jnp.bfloat16)


def widen(real_part, imag_part):
    return real_part.astype(jnp.float32) + 1j * imag_part.astype(jnp.float32)


def reference(raw_echoes, range_phase, band_start, band_weight, intersection_length, azimuth_rate):
    range_filter = jnp.exp(-1j * range_phase)

    def migrate_lines(component):
        padded = jnp.pad(component.astype(jnp.float32), ((0, 0), (0, 128)))
        summed = jnp.zeros(component.shape, jnp.float32)
        for tap_index in range(TAPS):
            picked = jnp.take(padded, band_start + tap_index, axis=1)
            summed = summed + band_weight[tap_index].astype(jnp.float32)[None, :] * picked
        return summed.astype(jnp.bfloat16)

    def range_section(echo_block):
        spectrum = jnp.fft.fft(widen(echo_block[0], echo_block[1]), axis=1) * range_filter[None, :]
        filt_real, filt_imag = round_pair(spectrum)
        lines = jnp.fft.ifft(widen(filt_real, filt_imag), axis=1)
        comp_real, comp_imag = round_pair(lines)
        return jnp.stack([migrate_lines(comp_real), migrate_lines(comp_imag)])

    migrated = lax.map(range_section, jnp.moveaxis(raw_echoes, 1, 0))
    head_lines = jnp.concatenate([migrated[1:, :, :OVLMAX], jnp.zeros_like(migrated[:1, :, :OVLMAX])], axis=0)
    pulses = jnp.arange(SUBP + OVLMAX)[:, None]
    inside = (pulses < SUBP) | (pulses - SUBP < intersection_length[None, :])
    doppler = jnp.arange(SUBP + OVLMAX)
    signed = jnp.where(2 * doppler >= SUBP + OVLMAX, doppler - (SUBP + OVLMAX), doppler).astype(jnp.float32)
    phase_angle = math.pi * azimuth_rate[None, :] * (signed * signed)[:, None] / (SUBP + OVLMAX)
    azimuth_filter = jnp.exp(-1j * phase_angle)

    def azimuth_section(operands):
        own_lines, next_lines = operands
        aperture = jnp.concatenate([own_lines, next_lines], axis=1)
        aperture = jnp.where(inside[None], aperture, jnp.zeros((), jnp.bfloat16))
        spectrum = jnp.fft.fft(widen(aperture[0], aperture[1]), axis=0) * azimuth_filter
        spec_real, spec_imag = round_pair(spectrum)
        image_pair = jnp.fft.ifft(widen(spec_real, spec_imag), axis=0)[:SUBP]
        image_real, image_imag = round_pair(image_pair)
        return jnp.stack([image_real, image_imag])

    images = lax.map(azimuth_section, (migrated, head_lines))
    return jnp.moveaxis(images, 0, 1)
```

```python
import functools
import math

import jax
import jax.numpy as jnp
import ml_dtypes
import numpy as np
from jax import lax
from jax.experimental import pallas as pl
from jax.experimental.pallas import tpu as pltpu
from jax.sharding import PartitionSpec as P

OVLMAX = 128
LANES = 128
SLAB = 16
VMEM_BYTES = 60 * 1024 * 1024


def fit_turns(power_start, terms):
    grid = 0.5 * np.cos(np.pi * (np.arange(4001) + 0.5) / 4001)
    basis = np.stack([grid ** (power_start + 2 * i) for i in range(terms)], axis=1)
    target = np.sin(2 * np.pi * grid) if power_start else np.cos(2 * np.pi * grid)
    return [float(c) for c in np.linalg.lstsq(basis, target, rcond=None)[0]]


SIN_TERMS = fit_turns(1, 7)
COS_TERMS = fit_turns(0, 7)


def turn_pair(turns):
    rest = turns - jnp.round(turns)
    square = rest * rest
    cosine = jnp.full_like(square, COS_TERMS[-1])
    sine = jnp.full_like(square, SIN_TERMS[-1])
    for c in COS_TERMS[-2::-1]:
        cosine = cosine * square + c
    for c in SIN_TERMS[-2::-1]:
        sine = sine * square + c
    return cosine, sine * rest


def unit_roots(rows, cols, length):
    angle = 2.0 * np.pi * (np.multiply.outer(rows, cols) % length) / length
    return np.cos(angle), np.sin(angle)


def left_table(cosine, sine, sign, scale=1.0):
    table = np.block([[cosine, -sign * sine], [sign * sine, cosine]]) * scale
    return table.astype(ml_dtypes.bfloat16)


def right_table(cosine, sine, sign, scale=1.0):
    table = np.block([[cosine, sign * sine], [-sign * sine, cosine]]) * scale
    return table.astype(ml_dtypes.bfloat16)


def dot(left, right):
    return jnp.dot(left, right, preferred_element_type=jnp.float32)


def range_kernel(plan, z_ref, raw_ref, phase_ref, starts_ref, weights_ref, twiddle_ref, first_ref, second_ref, third_ref, last_ref, *rest):
    first_pulse, pulses, bin_count, group_tiles, pair = plan
    out_refs = rest[: bin_count * len(group_tiles)]
    raw_v, slab_v, comp_v, filter_v, sems = rest[bin_count * len(group_tiles) :]
    heights = raw_ref.shape[-1] // LANES
    slabs = pulses // SLAB
    copies = [
        pltpu.make_async_copy(
            raw_ref.at[:, 0, pl.ds(first_pulse + SLAB * s, SLAB), :],
            raw_v.at[:, pl.ds(SLAB * s, SLAB), :],
            sems.at[s],
        )
        for s in range(slabs)
    ]
    for copy in copies:
        copy.start()
    cosine, sine = turn_pair(phase_ref[...].T * (0.5 / math.pi))
    filter_v[0] = cosine
    filter_v[1] = sine
    stride = comp_v.shape[0] // (heights + 1)
    comp_v[pl.ds(heights * stride, stride), :] = jnp.zeros((stride, LANES), jnp.float32)

    def slab_step(s, carry):
        row = pl.multiple_of(s * SLAB, SLAB)
        pltpu.make_async_copy(
            raw_ref.at[:, 0, pl.ds(pl.multiple_of(first_pulse + row, SLAB), SLAB), :],
            raw_v.at[:, pl.ds(row, SLAB), :],
            sems.at[s],
        ).wait()
        for comp in range(2):
            for a in range(heights):
                tile = raw_v[comp, pl.ds(row, SLAB), pl.ds(a * LANES, LANES)]
                slab_v[pl.ds((comp * heights + a) * SLAB, SLAB), :] = tile.astype(jnp.float32)

        def pulse_step(j, inner):
            columns = [
                slab_v[pl.ds(j * pair + i, 2 * heights, stride=SLAB), :].astype(jnp.bfloat16)
                for i in range(pair)
            ]
            part = dot(first_ref[...], jnp.concatenate(columns, axis=1))
            tw_cos, tw_sin = twiddle_ref[0], twiddle_ref[1]
            rows = []
            for i in range(pair):
                real = part[:heights, i * LANES : (i + 1) * LANES]
                imag = part[heights:, i * LANES : (i + 1) * LANES]
                rows.append(
                    jnp.concatenate(
                        [
                            (real * tw_cos + imag * tw_sin).astype(jnp.bfloat16),
                            (imag * tw_cos - real * tw_sin).astype(jnp.bfloat16),
                        ],
                        axis=1,
                    )
                )
            spectrum = dot(jnp.concatenate(rows, axis=0), second_ref[...])
            f_cos, f_sin = filter_v[0], filter_v[1]
            rows = []
            for i in range(pair):
                real = spectrum[i * heights : (i + 1) * heights, :LANES]
                imag = spectrum[i * heights : (i + 1) * heights, LANES:]
                rows.append(
                    jnp.concatenate(
                        [
                            (real * f_cos + imag * f_sin).astype(jnp.bfloat16),
                            (imag * f_cos - real * f_sin).astype(jnp.bfloat16),
                        ],
                        axis=1,
                    )
                )
            part = dot(jnp.concatenate(rows, axis=0), third_ref[...])
            columns = []
            for i in range(pair):
                real = part[i * heights : (i + 1) * heights, :LANES]
                imag = part[i * heights : (i + 1) * heights, LANES:]
                columns.append(
                    jnp.concatenate(
                        [
                            (real * tw_cos - imag * tw_sin).astype(jnp.bfloat16),
                            (imag * tw_cos + real * tw_sin).astype(jnp.bfloat16),
                        ],
                        axis=0,
                    )
                )
            line = dot(last_ref[...], jnp.concatenate(columns, axis=1))
            for i in range(pair):
                pulse = s * SLAB + j * pair + i
                for comp in range(2):
                    comp_v[pl.ds(comp * pulses + pulse, heights, stride=stride), :] = line[
                        comp * heights : (comp + 1) * heights, i * LANES : (i + 1) * LANES
                    ]
            return inner

        lax.fori_loop(0, SLAB // pair, pulse_step, 0)
        return carry

    lax.fori_loop(0, slabs, slab_step, 0)

    z = z_ref[0]
    tiles_per_device = heights // bin_count
    sub = lax.broadcasted_iota(jnp.int32, (8, LANES), 0)
    step = 0
    for mask in range(bin_count):
        tile_base = lax.bitwise_xor(z, mask) * tiles_per_device
        group_base = 0
        for group, tiles in enumerate(group_tiles):
            out_ref = out_refs[group * bin_count + mask]

            def migrate_step(t, carry, tile_base=tile_base, group_base=group_base, out_ref=out_ref):
                r = tile_base + group_base + t
                lane = pl.multiple_of(r * LANES, LANES)
                offset = starts_ref[pl.ds(r, 1), :] - lane
                low = lax.bitwise_and(offset, 7)
                taps = weights_ref[:, pl.ds(lane, LANES)].astype(jnp.float32)
                turned = lax.bitwise_and(sub - low, 7)
                weight = jnp.zeros((8, LANES), jnp.float32)
                for tap in range(8):
                    weight = jnp.where(turned == tap, taps[tap : tap + 1, :], weight)
                where_tile = lax.shift_right_logical(offset, 3) + jnp.where(sub < low, 1, 0)
                zero = jnp.zeros((8, LANES), jnp.float32)
                band = [
                    jnp.where(where_tile == i, weight, zero) if i < 26 else zero for i in range(2 * LANES // 8)
                ]
                band = jnp.concatenate(band, axis=0).astype(jnp.bfloat16)
                base = pl.multiple_of(r * stride, 8)
                window = jnp.concatenate(
                    [
                        comp_v[pl.ds(base, 2 * pulses), :].astype(jnp.bfloat16),
                        comp_v[pl.ds(base + stride, 2 * pulses), :].astype(jnp.bfloat16),
                    ],
                    axis=1,
                )
                value = dot(window, band).astype(jnp.bfloat16)
                at = pl.multiple_of(t * LANES, LANES)
                out_ref[0, :, pl.ds(at, LANES)] = value[:pulses]
                out_ref[1, :, pl.ds(at, LANES)] = value[pulses:]
                return carry

            lax.fori_loop(0, tiles, migrate_step, 0)
            group_base += tiles


def range_call(z, raw, phase, starts, weights, tables, first_pulse, pulses, bin_count, group_tiles):
    heights = raw.shape[-1] // LANES
    pair = 4
    stride = 2 * pulses + 8
    plan = (first_pulse, pulses, bin_count, tuple(group_tiles), pair)
    vmem = pl.BlockSpec(memory_space=pltpu.VMEM)
    return pl.pallas_call(
        functools.partial(range_kernel, plan),
        out_shape=[
            jax.ShapeDtypeStruct((2, pulses, tiles * LANES), jnp.bfloat16)
            for tiles in group_tiles
            for _ in range(bin_count)
        ],
        in_specs=[pl.BlockSpec(memory_space=pltpu.SMEM), pl.BlockSpec(memory_space=pl.ANY)] + [vmem] * (3 + len(tables)),
        out_specs=[vmem] * (bin_count * len(group_tiles)),
        scratch_shapes=[
            pltpu.VMEM((2, pulses, raw.shape[-1]), jnp.bfloat16),
            pltpu.VMEM((2 * heights * SLAB, LANES), jnp.float32),
            pltpu.VMEM(((heights + 1) * stride, LANES), jnp.float32),
            pltpu.VMEM((2, heights, LANES), jnp.float32),
            pltpu.SemaphoreType.DMA((pulses // SLAB,)),
        ],
        compiler_params=pltpu.CompilerParams(vmem_limit_bytes=VMEM_BYTES),
        cost_estimate=pl.CostEstimate(
            flops=90 * 10**6 * pulses, bytes_accessed=2 * 4 * pulses * raw.shape[-1], transcendentals=0
        ),
        name="range_lines",
    )(z, raw, phase, starts, weights, *tables)


def range_tables(width):
    heights = width // LANES
    first = unit_roots(np.arange(heights), np.arange(heights), heights)
    second = unit_roots(np.arange(LANES), np.arange(LANES), LANES)
    twiddle = np.stack(unit_roots(np.arange(heights), np.arange(LANES), width)).astype(np.float32)
    return (
        twiddle,
        left_table(*first, -1.0),
        right_table(*second, -1.0),
        right_table(*second, 1.0, 1.0 / LANES),
        left_table(*first, 1.0, 1.0 / heights),
    )


def head_kernel(sources, masks, z_ref, *rest):
    in_refs, out_ref, sem = rest[:masks], rest[masks], rest[masks + 1]
    z = z_ref[0]
    for source in range(sources):
        wanted = lax.bitwise_xor(z, source)
        for mask in range(masks):

            @pl.when(wanted == mask)
            def _(mask=mask, source=source):
                pltpu.make_async_copy(in_refs[mask], out_ref.at[source], sem.at[source]).start()

    for source in range(sources):
        pltpu.make_async_copy(in_refs[0], out_ref.at[source], sem.at[source]).wait()


def pick_head(z, pieces, sources):
    shape = pieces[0].shape
    return pl.pallas_call(
        functools.partial(head_kernel, sources, len(pieces)),
        out_shape=jax.ShapeDtypeStruct((sources,) + shape, jnp.bfloat16),
        in_specs=[pl.BlockSpec(memory_space=pltpu.SMEM)] + [pl.BlockSpec(memory_space=pl.ANY)] * len(pieces),
        out_specs=pl.BlockSpec(memory_space=pl.ANY),
        scratch_shapes=[pltpu.SemaphoreType.DMA((sources,))],
        compiler_params=pltpu.CompilerParams(vmem_limit_bytes=VMEM_BYTES),
        name="pick_head",
    )(z, *pieces)


def azimuth_kernel(plan, z_ref, length_ref, rate_ref, forward_ref, inverse_ref, *rest):
    parts, device_pulses, bin_count, lane_offset, width, tile, chained = plan
    count = len(parts) * (bin_count + 1)
    piece_refs = rest[:count]
    rest = rest[count + (1 if chained else 0) :]
    image_ref, aperture_v, spectrum_v, narrow_v, image_v, sems, out_sem = rest
    z = z_ref[0]
    lines = image_ref.shape[2]
    length = aperture_v.shape[1]
    half = length // 2
    copies = []
    at = 0
    for start, pulses, from_lane in parts:
        lanes = pl.ds(from_lane, width)
        for mask in range(bin_count):
            source = lax.bitwise_xor(z, mask)
            row = pl.multiple_of(source * device_pulses + start, SLAB)
            copies.append(
                pltpu.make_async_copy(
                    piece_refs[at].at[:, :, lanes], aperture_v.at[:, pl.ds(row, pulses), :], sems.at[len(copies)]
                )
            )
            at += 1
        heads = piece_refs[at]
        at += 1
        for source in range(heads.shape[0]):
            row = lines + source * device_pulses + start
            copies.append(
                pltpu.make_async_copy(
                    heads.at[source, :, :, lanes], aperture_v.at[:, pl.ds(row, pulses), :], sems.at[len(copies)]
                )
            )
    for copy in copies:
        copy.start()
    for copy in copies:
        copy.wait()

    block = 64
    for lane in range(0, width, tile):
        lanes = pl.ds(lane, tile)
        reach = length_ref[:, lanes]
        for row in range(lines, length, SLAB):
            pulse = lax.broadcasted_iota(jnp.int32, (SLAB, tile), 0) + (row - lines)
            inside = pulse < reach
            for comp in range(2):
                held = aperture_v[comp, pl.ds(row, SLAB), lanes].astype(jnp.float32)
                aperture_v[comp, pl.ds(row, SLAB), lanes] = jnp.where(inside, held, 0.0).astype(jnp.bfloat16)
        aperture = jnp.concatenate([aperture_v[0, :, lanes], aperture_v[1, :, lanes]], axis=0)
        spectrum_v[...] = dot(forward_ref[...], aperture)
        rate = rate_ref[:, lanes]

        def filter_rows(cosine, sine, row, size):
            real = spectrum_v[pl.ds(row, size), :]
            imag = spectrum_v[pl.ds(length + row, size), :]
            narrow_v[pl.ds(row, size), :] = (real * cosine + imag * sine).astype(jnp.bfloat16)
            narrow_v[pl.ds(length + row, size), :] = (imag * cosine - real * sine).astype(jnp.bfloat16)

        def filter_step(j, carry):
            row = pl.multiple_of(j * block, block)
            doppler = (lax.broadcasted_iota(jnp.int32, (block, tile), 0) + row).astype(jnp.float32)
            cosine, sine = turn_pair(rate * (doppler * doppler * (0.5 / length)))
            filter_rows(cosine, sine, row, block)
            doppler = jnp.where(doppler == 0.0, float(half), doppler)
            cosine, sine = turn_pair(rate * (doppler * doppler * (0.5 / length)))
            filter_rows(cosine, sine, pl.multiple_of(half + row, block), block)
            return carry

        lax.fori_loop(0, half // block, filter_step, 0)
        image = dot(inverse_ref[...], narrow_v[...]) * (1.0 / length)
        image_v[0, :, lanes] = image[:lines].astype(jnp.bfloat16)
        image_v[1, :, lanes] = image[lines:].astype(jnp.bfloat16)
    out = pltpu.make_async_copy(image_v, image_ref.at[:, 0, :, pl.ds(lane_offset, width)], out_sem)
    out.start()
    out.wait()


def azimuth_call(z, lengths, rates, tables, pieces, parts, device_pulses, bin_count, lane_offset, width, image_shape, image):
    vmem = pl.BlockSpec(memory_space=pltpu.VMEM)
    lines = image_shape[2]
    length = lines + OVLMAX
    tile = 2 * LANES if width % (2 * LANES) == 0 else LANES
    chained = image is not None
    plan = (tuple(parts), device_pulses, bin_count, lane_offset, width, tile, chained)
    sources = pieces[bin_count].shape[0]
    lengths = lax.slice_in_dim(lengths, lane_offset, lane_offset + width)[None]
    rates = lax.slice_in_dim(rates, lane_offset, lane_offset + width)[None]
    operands = [z, lengths, rates, *tables, *pieces] + ([image] if chained else [])
    any_spec = pl.BlockSpec(memory_space=pl.ANY)
    return pl.pallas_call(
        functools.partial(azimuth_kernel, plan),
        out_shape=jax.ShapeDtypeStruct(image_shape, jnp.bfloat16),
        in_specs=[pl.BlockSpec(memory_space=pltpu.SMEM)] + [vmem] * 4 + [any_spec] * (len(operands) - 5),
        out_specs=any_spec,
        scratch_shapes=[
            pltpu.VMEM((2, length, width), jnp.bfloat16),
            pltpu.VMEM((2 * length, tile), jnp.float32),
            pltpu.VMEM((2 * length, tile), jnp.bfloat16),
            pltpu.VMEM((2, lines, width), jnp.bfloat16),
            pltpu.SemaphoreType.DMA((len(parts) * (bin_count + sources),)),
            pltpu.SemaphoreType.DMA,
        ],
        input_output_aliases={len(operands) - 1: 0} if chained else {},
        compiler_params=pltpu.CompilerParams(vmem_limit_bytes=VMEM_BYTES),
        cost_estimate=pl.CostEstimate(
            flops=2 * width * (2 * length) * (2 * length + 2 * lines),
            bytes_accessed=4 * (2 * lines + OVLMAX) * width,
            transcendentals=0,
        ),
        name="azimuth_bins",
    )(*operands)


def azimuth_tables(lines):
    length = lines + OVLMAX
    half = length // 2
    order = np.concatenate([np.arange(half), [half], length - np.arange(1, half)])
    forward = left_table(*unit_roots(order, np.arange(length), length), -1.0)
    inverse = left_table(*unit_roots(np.arange(lines), order, length), 1.0)
    return forward, inverse


def exchanged(value, mask):
    count = lax.axis_size("bins")
    return lax.ppermute(value, "bins", [(s, s ^ mask) for s in range(count)]) if mask else value


def passed_back(value):
    count = lax.axis_size("az")
    return lax.ppermute(value, "az", [(s, s - 1) for s in range(1, count)])


def split_tiles(tiles):
    small = max(1, tiles // 8)
    big = max(1, (tiles - 2 * small) // 2)
    shares = []
    while sum(shares) + big + 2 * small <= tiles:
        shares.append(big)
    rest = tiles - sum(shares) - 2 * small
    if rest > 0:
        shares.append(rest)
    return shares + [small, small]


def shards(raw_echoes, range_phase, band_start, band_weight, intersection_length, azimuth_rate):
    bin_count = lax.axis_size("bins")
    width = raw_echoes.shape[-1]
    heights = width // LANES
    device_pulses = raw_echoes.shape[2]
    lines = device_pulses * bin_count
    device_bins = width // bin_count
    device_tiles = device_bins // LANES
    z = lax.axis_index("bins").astype(jnp.int32).reshape(1)
    phase = range_phase.reshape(LANES, heights)
    starts = band_start.reshape(heights, LANES)
    tables = [jnp.asarray(t) for t in range_tables(width)]
    sources = max(1, OVLMAX // device_pulses)
    first = max(SLAB, device_pulses // 4 // SLAB * SLAB)
    shares = split_tiles(device_tiles)

    def line_call(at, pulses, tiles):
        return range_call(z, raw_echoes, phase, starts, band_weight, tables, at, pulses, bin_count, tiles)

    early = line_call(0, first, [device_tiles])
    early = [exchanged(v, m) for m, v in enumerate(early)]
    late = line_call(first, device_pulses - first, shares)
    early_head = passed_back(pick_head(z, early, sources))
    late = [
        [exchanged(v, m) for m, v in enumerate(late[g * bin_count : (g + 1) * bin_count])] for g in range(len(shares))
    ]
    late_heads = [passed_back(pick_head(z, pieces, sources)) for pieces in late]
    az_tables = [jnp.asarray(t) for t in azimuth_tables(lines)]
    image_shape = (2, 1, lines, device_bins)
    image = None
    offset = 0
    for share, pieces, head in zip(shares, late, late_heads):
        image = azimuth_call(
            z,
            intersection_length,
            azimuth_rate,
            az_tables,
            [*early, early_head, *pieces, head],
            [(0, first, offset), (first, device_pulses - first, 0)],
            device_pulses,
            bin_count,
            offset,
            share * LANES,
            image_shape,
            image,
        )
        offset += share * LANES
    return image


def solution(mesh):
    in_specs = (P(None, ("scene", "az"), "bins", None), P(), P(), P(), P("bins"), P("bins"))
    out_specs = P(None, ("scene", "az"), None, "bins")
    return jax.shard_map(shards, mesh=mesh, in_specs=in_specs, out_specs=out_specs, check_vma=False)
```

```python
import functools
import math

import jax
import jax.numpy as jnp
import ml_dtypes
import numpy as np
from jax import lax
from jax.experimental import pallas as pl
from jax.experimental.pallas import tpu as pltpu
from jax.sharding import PartitionSpec as P

OVLMAX = 128
LANES = 128
SLAB = 16
COST = 1000
FIRST = 4
ENDS = (10 / 32, 18 / 32, 24 / 32, 28 / 32)
VMEM_BYTES = 60 * 1024 * 1024


def fit_turns(power_start, terms):
    grid = 0.5 * np.cos(np.pi * (np.arange(4001) + 0.5) / 4001)
    basis = np.stack([grid ** (power_start + 2 * i) for i in range(terms)], axis=1)
    target = np.sin(2 * np.pi * grid) if power_start else np.cos(2 * np.pi * grid)
    return [float(c) for c in np.linalg.lstsq(basis, target, rcond=None)[0]]


SIN_TERMS = fit_turns(1, 7)
COS_TERMS = fit_turns(0, 7)


def turn_pair(turns):
    rest = turns - jnp.round(turns)
    square = rest * rest
    cosine = jnp.full_like(square, COS_TERMS[-1])
    sine = jnp.full_like(square, SIN_TERMS[-1])
    for c in COS_TERMS[-2::-1]:
        cosine = cosine * square + c
    for c in SIN_TERMS[-2::-1]:
        sine = sine * square + c
    return cosine, sine * rest


def unit_roots(rows, cols, length):
    angle = 2.0 * np.pi * (np.multiply.outer(rows, cols) % length) / length
    return np.cos(angle), np.sin(angle)


def left_table(cosine, sine, sign, scale=1.0):
    table = np.block([[cosine, -sign * sine], [sign * sine, cosine]]) * scale
    return table.astype(ml_dtypes.bfloat16)


def right_table(cosine, sine, sign, scale=1.0):
    table = np.block([[cosine, sign * sine], [-sign * sine, cosine]]) * scale
    return table.astype(ml_dtypes.bfloat16)


def dot(left, right):
    return jnp.dot(left, right, preferred_element_type=jnp.float32)


def range_kernel(plan, z_ref, raw_ref, phase_ref, starts_ref, weights_ref, twiddle_ref, first_ref, second_ref, third_ref, last_ref, *rest):
    first_pulse, pulses, bin_count, group_tiles, pair = plan
    out_refs = rest[: bin_count * len(group_tiles)]
    raw_v, slab_v, comp_v, filter_v, sems = rest[bin_count * len(group_tiles) :]
    heights = raw_ref.shape[-1] // LANES
    slabs = pulses // SLAB
    copies = [
        pltpu.make_async_copy(
            raw_ref.at[:, 0, pl.ds(first_pulse + SLAB * s, SLAB), :],
            raw_v.at[:, pl.ds(SLAB * s, SLAB), :],
            sems.at[s],
        )
        for s in range(slabs)
    ]
    for copy in copies:
        copy.start()
    cosine, sine = turn_pair(phase_ref[...].T * (0.5 / math.pi))
    filter_v[0] = cosine
    filter_v[1] = sine
    stride = comp_v.shape[0] // (heights + 1)
    comp_v[pl.ds(heights * stride, stride), :] = jnp.zeros((stride, LANES), jnp.float32)

    def slab_step(s, carry):
        row = pl.multiple_of(s * SLAB, SLAB)
        pltpu.make_async_copy(
            raw_ref.at[:, 0, pl.ds(pl.multiple_of(first_pulse + row, SLAB), SLAB), :],
            raw_v.at[:, pl.ds(row, SLAB), :],
            sems.at[s],
        ).wait()
        for comp in range(2):
            for a in range(heights):
                tile = raw_v[comp, pl.ds(row, SLAB), pl.ds(a * LANES, LANES)]
                slab_v[pl.ds((comp * heights + a) * SLAB, SLAB), :] = tile.astype(jnp.float32)

        def pulse_step(j, inner):
            columns = [
                slab_v[pl.ds(j * pair + i, 2 * heights, stride=SLAB), :].astype(jnp.bfloat16)
                for i in range(pair)
            ]
            part = dot(first_ref[...], jnp.concatenate(columns, axis=1))
            tw_cos, tw_sin = twiddle_ref[0], twiddle_ref[1]
            rows = []
            for i in range(pair):
                real = part[:heights, i * LANES : (i + 1) * LANES]
                imag = part[heights:, i * LANES : (i + 1) * LANES]
                rows.append(
                    jnp.concatenate(
                        [
                            (real * tw_cos + imag * tw_sin).astype(jnp.bfloat16),
                            (imag * tw_cos - real * tw_sin).astype(jnp.bfloat16),
                        ],
                        axis=1,
                    )
                )
            spectrum = dot(jnp.concatenate(rows, axis=0), second_ref[...])
            f_cos, f_sin = filter_v[0], filter_v[1]
            rows = []
            for i in range(pair):
                real = spectrum[i * heights : (i + 1) * heights, :LANES]
                imag = spectrum[i * heights : (i + 1) * heights, LANES:]
                rows.append(
                    jnp.concatenate(
                        [
                            (real * f_cos + imag * f_sin).astype(jnp.bfloat16),
                            (imag * f_cos - real * f_sin).astype(jnp.bfloat16),
                        ],
                        axis=1,
                    )
                )
            part = dot(jnp.concatenate(rows, axis=0), third_ref[...])
            columns = []
            for i in range(pair):
                real = part[i * heights : (i + 1) * heights, :LANES]
                imag = part[i * heights : (i + 1) * heights, LANES:]
                columns.append(
                    jnp.concatenate(
                        [
                            (real * tw_cos - imag * tw_sin).astype(jnp.bfloat16),
                            (imag * tw_cos + real * tw_sin).astype(jnp.bfloat16),
                        ],
                        axis=0,
                    )
                )
            line = dot(last_ref[...], jnp.concatenate(columns, axis=1))
            for i in range(pair):
                pulse = s * SLAB + j * pair + i
                for comp in range(2):
                    comp_v[pl.ds(comp * pulses + pulse, heights, stride=stride), :] = line[
                        comp * heights : (comp + 1) * heights, i * LANES : (i + 1) * LANES
                    ]
            return inner

        lax.fori_loop(0, SLAB // pair, pulse_step, 0, unroll=True)
        return carry

    lax.fori_loop(0, slabs, slab_step, 0)

    z = z_ref[0]
    tiles_per_device = heights // bin_count
    sub = lax.broadcasted_iota(jnp.int32, (8, LANES), 0)
    step = 0
    for mask in range(bin_count):
        tile_base = lax.bitwise_xor(z, mask) * tiles_per_device
        group_base = 0
        for group, tiles in enumerate(group_tiles):
            out_ref = out_refs[group * bin_count + mask]

            def migrate_step(t, carry, tile_base=tile_base, group_base=group_base, out_ref=out_ref):
                r = tile_base + group_base + t
                lane = pl.multiple_of(r * LANES, LANES)
                offset = starts_ref[pl.ds(r, 1), :] - lane
                low = lax.bitwise_and(offset, 7)
                taps = weights_ref[:, pl.ds(lane, LANES)].astype(jnp.float32)
                turned = lax.bitwise_and(sub - low, 7)
                weight = jnp.zeros((8, LANES), jnp.float32)
                for tap in range(8):
                    weight = jnp.where(turned == tap, taps[tap : tap + 1, :], weight)
                where_tile = lax.shift_right_logical(offset, 3) + jnp.where(sub < low, 1, 0)
                zero = jnp.zeros((8, LANES), jnp.float32)
                band = [
                    jnp.where(where_tile == i, weight, zero) if i < 26 else zero for i in range(2 * LANES // 8)
                ]
                band = jnp.concatenate(band, axis=0).astype(jnp.bfloat16)
                base = pl.multiple_of(r * stride, 8)
                window = jnp.concatenate(
                    [
                        comp_v[pl.ds(base, 2 * pulses), :].astype(jnp.bfloat16),
                        comp_v[pl.ds(base + stride, 2 * pulses), :].astype(jnp.bfloat16),
                    ],
                    axis=1,
                )
                value = dot(window, band).astype(jnp.bfloat16)
                at = pl.multiple_of(t * LANES, LANES)
                out_ref[0, :, pl.ds(at, LANES)] = value[:pulses]
                out_ref[1, :, pl.ds(at, LANES)] = value[pulses:]
                return carry

            lax.fori_loop(0, tiles, migrate_step, 0, unroll=math.gcd(tiles, 16) if tiles > 16 else tiles)
            group_base += tiles


def range_call(z, raw, phase, starts, weights, tables, first_pulse, pulses, bin_count, group_tiles):
    heights = raw.shape[-1] // LANES
    pair = 4
    stride = 2 * pulses + 8
    plan = (first_pulse, pulses, bin_count, tuple(group_tiles), pair)
    vmem = pl.BlockSpec(memory_space=pltpu.VMEM)
    return pl.pallas_call(
        functools.partial(range_kernel, plan),
        out_shape=[
            jax.ShapeDtypeStruct((2, pulses, tiles * LANES), jnp.bfloat16)
            for tiles in group_tiles
            for _ in range(bin_count)
        ],
        in_specs=[pl.BlockSpec(memory_space=pltpu.SMEM), pl.BlockSpec(memory_space=pl.ANY)] + [vmem] * (3 + len(tables)),
        out_specs=[vmem] * (bin_count * len(group_tiles)),
        scratch_shapes=[
            pltpu.VMEM((2, pulses, raw.shape[-1]), jnp.bfloat16),
            pltpu.VMEM((2 * heights * SLAB, LANES), jnp.float32),
            pltpu.VMEM(((heights + 1) * stride, LANES), jnp.float32),
            pltpu.VMEM((2, heights, LANES), jnp.float32),
            pltpu.SemaphoreType.DMA((pulses // SLAB,)),
        ],
        compiler_params=pltpu.CompilerParams(vmem_limit_bytes=VMEM_BYTES),
        cost_estimate=pl.CostEstimate(
            flops=COST, bytes_accessed=COST, transcendentals=0
        ),
        name="range_lines",
    )(z, raw, phase, starts, weights, *tables)


def range_tables(width):
    heights = width // LANES
    first = unit_roots(np.arange(heights), np.arange(heights), heights)
    second = unit_roots(np.arange(LANES), np.arange(LANES), LANES)
    twiddle = np.stack(unit_roots(np.arange(heights), np.arange(LANES), width)).astype(np.float32)
    return (
        twiddle,
        left_table(*first, -1.0),
        right_table(*second, -1.0),
        right_table(*second, 1.0, 1.0 / LANES),
        left_table(*first, 1.0, 1.0 / heights),
    )


def head_kernel(sources, masks, z_ref, *rest):
    in_refs, out_ref, sem = rest[:masks], rest[masks], rest[masks + 1]
    z = z_ref[0]
    for source in range(sources):
        wanted = lax.bitwise_xor(z, source)
        for mask in range(masks):

            @pl.when(wanted == mask)
            def _(mask=mask, source=source):
                pltpu.make_async_copy(in_refs[mask], out_ref.at[source], sem.at[source]).start()

    for source in range(sources):
        pltpu.make_async_copy(in_refs[0], out_ref.at[source], sem.at[source]).wait()


def pick_head(z, pieces, sources):
    shape = pieces[0].shape
    return pl.pallas_call(
        functools.partial(head_kernel, sources, len(pieces)),
        out_shape=jax.ShapeDtypeStruct((sources,) + shape, jnp.bfloat16),
        in_specs=[pl.BlockSpec(memory_space=pltpu.SMEM)] + [pl.BlockSpec(memory_space=pl.ANY)] * len(pieces),
        out_specs=pl.BlockSpec(memory_space=pltpu.VMEM),
        scratch_shapes=[pltpu.SemaphoreType.DMA((sources,))],
        compiler_params=pltpu.CompilerParams(vmem_limit_bytes=VMEM_BYTES),
        name="pick_head",
    )(z, *pieces)


def azimuth_kernel(plan, z_ref, length_ref, rate_ref, forward_hbm, inverse_hbm, *rest):
    parts, device_pulses, bin_count, lane_offset, width, tile, chained = plan
    count = len(parts) * (bin_count + 1)
    piece_refs = rest[:count]
    rest = rest[count + (1 if chained else 0) :]
    image_ref, forward_ref, inverse_ref, aperture_v, spectrum_v, narrow_v, image_v, sems, table_sems, out_sem = rest
    z = z_ref[0]
    lines = image_ref.shape[2]
    length = aperture_v.shape[1]
    half = length // 2
    copies = []
    at = 0
    for start, pulses, from_lane in parts:
        lanes = pl.ds(from_lane, width)
        for mask in range(bin_count):
            source = lax.bitwise_xor(z, mask)
            row = pl.multiple_of(source * device_pulses + start, SLAB)
            copies.append(
                pltpu.make_async_copy(
                    piece_refs[at].at[:, :, lanes], aperture_v.at[:, pl.ds(row, pulses), :], sems.at[len(copies)]
                )
            )
            at += 1
        heads = piece_refs[at]
        at += 1
        for source in range(heads.shape[0]):
            row = lines + source * device_pulses + start
            copies.append(
                pltpu.make_async_copy(
                    heads.at[source, :, :, lanes], aperture_v.at[:, pl.ds(row, pulses), :], sems.at[len(copies)]
                )
            )
    tables = [
        pltpu.make_async_copy(forward_hbm, forward_ref, table_sems.at[0]),
        pltpu.make_async_copy(inverse_hbm, inverse_ref, table_sems.at[1]),
    ]
    for copy in copies + tables:
        copy.start()
    for copy in copies:
        copy.wait()

    def row_of(ref, lane):
        first = (lane_offset + lane) // LANES
        return jnp.concatenate([ref[pl.ds(first + i, 1), :] for i in range(tile // LANES)], axis=1)

    block = 64
    outs = []
    for lane in range(0, width, tile):
        lanes = pl.ds(lane, tile)
        reach = row_of(length_ref, lane)
        for row in range(lines, length, SLAB):
            pulse = lax.broadcasted_iota(jnp.int32, (SLAB, tile), 0) + (row - lines)
            inside = pulse < reach
            for comp in range(2):
                held = aperture_v[comp, pl.ds(row, SLAB), lanes].astype(jnp.float32)
                aperture_v[comp, pl.ds(row, SLAB), lanes] = jnp.where(inside, held, 0.0).astype(jnp.bfloat16)
        real, imag = aperture_v[0, :, lanes], aperture_v[1, :, lanes]
        pair = jnp.concatenate(
            [jnp.concatenate([real, imag], axis=0), jnp.concatenate([imag, -real], axis=0)], axis=1
        )
        if lane == 0:
            tables[0].wait()
        spectrum_v[...] = dot(forward_ref[...], pair)
        rate = row_of(rate_ref, lane)

        def filter_rows(cosine, sine, row, size):
            real = spectrum_v[pl.ds(row, size), :tile]
            imag = spectrum_v[pl.ds(row, size), tile:]
            turned_real = (real * cosine + imag * sine).astype(jnp.bfloat16)
            turned_imag = (imag * cosine - real * sine).astype(jnp.bfloat16)
            narrow_v[pl.ds(row, size), :tile] = turned_real
            narrow_v[pl.ds(row, size), tile:] = turned_imag
            narrow_v[pl.ds(length + row, size), :tile] = -turned_imag
            narrow_v[pl.ds(length + row, size), tile:] = turned_real

        def doppler_phase(doppler):
            return turn_pair(rate * (doppler * doppler * (0.5 / length)))

        for row in range(0, half, block):
            doppler = (lax.broadcasted_iota(jnp.int32, (block, tile), 0) + row).astype(jnp.float32)
            cosine, sine = doppler_phase(doppler)
            filter_rows(cosine, sine, row, block)
            if row == 0:
                top = doppler[:SLAB]
                top_cos, top_sin = doppler_phase(jnp.where(top == 0.0, float(half), top))
                filter_rows(top_cos, top_sin, half, SLAB)
                filter_rows(cosine[SLAB:], sine[SLAB:], half + SLAB, block - SLAB)
            else:
                filter_rows(cosine, sine, half + row, block)

        if lane == 0:
            tables[1].wait()
        image = dot(inverse_ref[...], narrow_v[...]) * (1.0 / length)
        image_v[0, :, lanes] = image[:, :tile].astype(jnp.bfloat16)
        image_v[1, :, lanes] = image[:, tile:].astype(jnp.bfloat16)
        outs.append(
            pltpu.make_async_copy(
                image_v.at[:, :, lanes],
                image_ref.at[:, 0, :, pl.ds(lane_offset + lane, tile)],
                out_sem.at[lane // tile],
            )
        )
        outs[-1].start()
    for out in outs:
        out.wait()


def azimuth_call(z, lengths, rates, tables, pieces, parts, device_pulses, bin_count, lane_offset, width, image_shape, image):
    vmem = pl.BlockSpec(memory_space=pltpu.VMEM)
    lines = image_shape[2]
    length = lines + OVLMAX
    tile = next(t * LANES for t in (4, 3, 2, 1) if width % (t * LANES) == 0)
    chained = image is not None
    plan = (tuple(parts), device_pulses, bin_count, lane_offset, width, tile, chained)
    sources = pieces[bin_count].shape[0]
    operands = [z, lengths, rates, *tables, *pieces] + ([image] if chained else [])
    any_spec = pl.BlockSpec(memory_space=pl.ANY)
    return pl.pallas_call(
        functools.partial(azimuth_kernel, plan),
        out_shape=jax.ShapeDtypeStruct(image_shape, jnp.bfloat16),
        in_specs=[pl.BlockSpec(memory_space=pltpu.SMEM)] + [vmem] * 2 + [any_spec] * (len(operands) - 3),
        out_specs=any_spec,
        scratch_shapes=[
            pltpu.VMEM(tables[0].shape, jnp.bfloat16),
            pltpu.VMEM(tables[1].shape, jnp.bfloat16),
            pltpu.VMEM((2, length, width), jnp.bfloat16),
            pltpu.VMEM((length, 2 * tile), jnp.float32),
            pltpu.VMEM((2 * length, 2 * tile), jnp.bfloat16),
            pltpu.VMEM((2, lines, width), jnp.bfloat16),
            pltpu.SemaphoreType.DMA((len(parts) * (bin_count + sources),)),
            pltpu.SemaphoreType.DMA((2,)),
            pltpu.SemaphoreType.DMA((width // tile,)),
        ],
        input_output_aliases={len(operands) - 1: 0} if chained else {},
        compiler_params=pltpu.CompilerParams(vmem_limit_bytes=VMEM_BYTES),
        cost_estimate=pl.CostEstimate(
            flops=COST,
            bytes_accessed=COST,
            transcendentals=0,
        ),
        name="azimuth_bins",
    )(*operands)


def azimuth_tables(lines):
    length = lines + OVLMAX
    half = length // 2
    order = np.concatenate([np.arange(half), [half], length - np.arange(1, half)])
    forward = np.concatenate(unit_roots(order, np.arange(length), length), axis=1)
    inverse = np.concatenate(unit_roots(np.arange(lines), order, length), axis=1)
    return forward.astype(ml_dtypes.bfloat16), inverse.astype(ml_dtypes.bfloat16)


def exchanged(value, mask):
    count = lax.axis_size("bins")
    return lax.ppermute(value, "bins", [(s, s ^ mask) for s in range(count)]) if mask else value


def passed_back(value):
    count = lax.axis_size("az")
    return lax.ppermute(value, "az", [(s, s - 1) for s in range(1, count)])


def split_tiles(tiles):
    ends = sorted({max(1, round(tiles * f)) for f in ENDS} | {tiles})
    return [b - a for a, b in zip([0] + ends[:-1], ends)]


def shards(raw_echoes, range_phase, band_start, band_weight, intersection_length, azimuth_rate):
    bin_count = lax.axis_size("bins")
    width = raw_echoes.shape[-1]
    heights = width // LANES
    device_pulses = raw_echoes.shape[2]
    lines = device_pulses * bin_count
    device_bins = width // bin_count
    device_tiles = device_bins // LANES
    z = lax.axis_index("bins").astype(jnp.int32).reshape(1)
    phase = range_phase.reshape(LANES, heights)
    starts = band_start.reshape(heights, LANES)
    tables = [jnp.asarray(t) for t in range_tables(width)]
    sources = max(1, OVLMAX // device_pulses)
    first = max(SLAB, device_pulses // FIRST // SLAB * SLAB)
    shares = split_tiles(device_tiles)

    def line_call(turn, at, pulses, tiles):
        return range_call(turn, raw_echoes, phase, starts, band_weight, tables, at, pulses, bin_count, tiles)

    early = line_call(z, 0, first, [device_tiles])
    late_z, early = lax.optimization_barrier((z, early))
    early = [exchanged(v, m) for m, v in enumerate(early)]
    late = line_call(late_z, first, device_pulses - first, shares)
    early, late = lax.optimization_barrier((early, late))
    early_head = passed_back(pick_head(z, early, sources))
    late = [
        [exchanged(v, m) for m, v in enumerate(late[g * bin_count : (g + 1) * bin_count])] for g in range(len(shares))
    ]
    az_tables = [jnp.asarray(t) for t in azimuth_tables(lines)]
    image_shape = (2, 1, lines, device_bins)
    lengths = intersection_length.reshape(device_tiles, LANES)
    rates = azimuth_rate.reshape(device_tiles, LANES)
    offset = 0
    image = None
    head = passed_back(pick_head(z, late[0], sources))
    for g, share in enumerate(shares):
        pieces, next_head, turn = late[g], None, z
        if g + 1 < len(shares):
            if image is not None:
                turn, image = lax.optimization_barrier((z, image))
            ahead = pick_head(turn, late[g + 1], sources)
            next_head = passed_back(ahead)
            turn, _ = lax.optimization_barrier((z, ahead))
        image = azimuth_call(
            turn,
            lengths,
            rates,
            az_tables,
            [*early, early_head, *pieces, head],
            [(0, first, offset), (first, device_pulses - first, 0)],
            device_pulses,
            bin_count,
            offset,
            share * LANES,
            image_shape,
            image,
        )
        head = next_head
        offset += share * LANES
    return image


def solution(mesh):
    in_specs = (P(None, ("scene", "az"), "bins", None), P(), P(), P(), P("bins"), P("bins"))
    out_specs = P(None, ("scene", "az"), None, "bins")
    return jax.shard_map(shards, mesh=mesh, in_specs=in_specs, out_specs=out_specs, check_vma=False)
```

```python
import functools
import math

import jax
import jax.numpy as jnp
import ml_dtypes
import numpy as np
from jax import lax
from jax.experimental import pallas as pl
from jax.experimental.pallas import tpu as pltpu
from jax.sharding import PartitionSpec as P

OVLMAX = 128
LANES = 128
SLAB = 16
COST = 1000
FIRST = 8
ENDS = (10 / 32, 18 / 32, 24 / 32, 28 / 32)
VMEM_BYTES = 60 * 1024 * 1024


def fit_turns(power_start, terms):
    grid = 0.5 * np.cos(np.pi * (np.arange(4001) + 0.5) / 4001)
    basis = np.stack([grid ** (power_start + 2 * i) for i in range(terms)], axis=1)
    target = np.sin(2 * np.pi * grid) if power_start else np.cos(2 * np.pi * grid)
    return [float(c) for c in np.linalg.lstsq(basis, target, rcond=None)[0]]


SIN_TERMS = fit_turns(1, 7)
COS_TERMS = fit_turns(0, 7)


def turn_pair(turns):
    rest = turns - jnp.round(turns)
    square = rest * rest
    cosine = jnp.full_like(square, COS_TERMS[-1])
    sine = jnp.full_like(square, SIN_TERMS[-1])
    for c in COS_TERMS[-2::-1]:
        cosine = cosine * square + c
    for c in SIN_TERMS[-2::-1]:
        sine = sine * square + c
    return cosine, sine * rest


def unit_roots(rows, cols, length):
    angle = 2.0 * np.pi * (np.multiply.outer(rows, cols) % length) / length
    return np.cos(angle), np.sin(angle)


def left_table(cosine, sine, sign, scale=1.0):
    table = np.block([[cosine, -sign * sine], [sign * sine, cosine]]) * scale
    return table.astype(ml_dtypes.bfloat16)


def right_table(cosine, sine, sign, scale=1.0):
    table = np.block([[cosine, sign * sine], [-sign * sine, cosine]]) * scale
    return table.astype(ml_dtypes.bfloat16)


def dot(left, right):
    return jnp.dot(left, right, preferred_element_type=jnp.float32)


def range_kernel(plan, z_ref, raw_ref, phase_ref, starts_ref, weights_ref, twiddle_ref, first_ref, second_ref, third_ref, last_ref, *rest):
    first_pulse, pulses, bin_count, group_tiles, pair = plan
    out_refs = rest[: bin_count * len(group_tiles)]
    raw_v, slab_v, comp_v, filter_v, sems = rest[bin_count * len(group_tiles) :]
    heights = raw_ref.shape[-1] // LANES
    slabs = pulses // SLAB
    copies = [
        pltpu.make_async_copy(
            raw_ref.at[:, 0, pl.ds(first_pulse + SLAB * s, SLAB), :],
            raw_v.at[:, pl.ds(SLAB * s, SLAB), :],
            sems.at[s],
        )
        for s in range(slabs)
    ]
    for copy in copies:
        copy.start()
    cosine, sine = turn_pair(phase_ref[...].T * (0.5 / math.pi))
    filter_v[0] = cosine
    filter_v[1] = sine
    stride = comp_v.shape[0] // (heights + 1)
    comp_v[pl.ds(heights * stride, stride), :] = jnp.zeros((stride, LANES), jnp.float32)

    def slab_step(s, carry):
        row = pl.multiple_of(s * SLAB, SLAB)
        pltpu.make_async_copy(
            raw_ref.at[:, 0, pl.ds(pl.multiple_of(first_pulse + row, SLAB), SLAB), :],
            raw_v.at[:, pl.ds(row, SLAB), :],
            sems.at[s],
        ).wait()
        for comp in range(2):
            for a in range(heights):
                tile = raw_v[comp, pl.ds(row, SLAB), pl.ds(a * LANES, LANES)]
                slab_v[pl.ds((comp * heights + a) * SLAB, SLAB), :] = tile.astype(jnp.float32)

        def pulse_step(j, inner):
            columns = [
                slab_v[pl.ds(j * pair + i, 2 * heights, stride=SLAB), :].astype(jnp.bfloat16)
                for i in range(pair)
            ]
            part = dot(first_ref[...], jnp.concatenate(columns, axis=1))
            tw_cos, tw_sin = twiddle_ref[0], twiddle_ref[1]
            rows = []
            for i in range(pair):
                real = part[:heights, i * LANES : (i + 1) * LANES]
                imag = part[heights:, i * LANES : (i + 1) * LANES]
                rows.append(
                    jnp.concatenate(
                        [
                            (real * tw_cos + imag * tw_sin).astype(jnp.bfloat16),
                            (imag * tw_cos - real * tw_sin).astype(jnp.bfloat16),
                        ],
                        axis=1,
                    )
                )
            spectrum = dot(jnp.concatenate(rows, axis=0), second_ref[...])
            f_cos, f_sin = filter_v[0], filter_v[1]
            rows = []
            for i in range(pair):
                real = spectrum[i * heights : (i + 1) * heights, :LANES]
                imag = spectrum[i * heights : (i + 1) * heights, LANES:]
                rows.append(
                    jnp.concatenate(
                        [
                            (real * f_cos + imag * f_sin).astype(jnp.bfloat16),
                            (imag * f_cos - real * f_sin).astype(jnp.bfloat16),
                        ],
                        axis=1,
                    )
                )
            part = dot(jnp.concatenate(rows, axis=0), third_ref[...])
            columns = []
            for i in range(pair):
                real = part[i * heights : (i + 1) * heights, :LANES]
                imag = part[i * heights : (i + 1) * heights, LANES:]
                columns.append(
                    jnp.concatenate(
                        [
                            (real * tw_cos - imag * tw_sin).astype(jnp.bfloat16),
                            (imag * tw_cos + real * tw_sin).astype(jnp.bfloat16),
                        ],
                        axis=0,
                    )
                )
            line = dot(last_ref[...], jnp.concatenate(columns, axis=1))
            for i in range(pair):
                pulse = s * SLAB + j * pair + i
                for comp in range(2):
                    comp_v[pl.ds(comp * pulses + pulse, heights, stride=stride), :] = line[
                        comp * heights : (comp + 1) * heights, i * LANES : (i + 1) * LANES
                    ]
            return inner

        lax.fori_loop(0, SLAB // pair, pulse_step, 0, unroll=True)
        return carry

    lax.fori_loop(0, slabs, slab_step, 0)

    z = z_ref[0]
    tiles_per_device = heights // bin_count
    sub = lax.broadcasted_iota(jnp.int32, (8, LANES), 0)
    step = 0
    for mask in range(bin_count):
        tile_base = lax.bitwise_xor(z, mask) * tiles_per_device
        group_base = 0
        for group, tiles in enumerate(group_tiles):
            out_ref = out_refs[group * bin_count + mask]

            def migrate_step(t, carry, tile_base=tile_base, group_base=group_base, out_ref=out_ref):
                r = tile_base + group_base + t
                lane = pl.multiple_of(r * LANES, LANES)
                offset = starts_ref[pl.ds(r, 1), :] - lane
                low = lax.bitwise_and(offset, 7)
                taps = weights_ref[:, pl.ds(lane, LANES)].astype(jnp.float32)
                turned = lax.bitwise_and(sub - low, 7)
                weight = jnp.zeros((8, LANES), jnp.float32)
                for tap in range(8):
                    weight = jnp.where(turned == tap, taps[tap : tap + 1, :], weight)
                where_tile = lax.shift_right_logical(offset, 3) + jnp.where(sub < low, 1, 0)
                zero = jnp.zeros((8, LANES), jnp.float32)
                band = [
                    jnp.where(where_tile == i, weight, zero) if i < 26 else zero for i in range(2 * LANES // 8)
                ]
                band = jnp.concatenate(band, axis=0).astype(jnp.bfloat16)
                base = pl.multiple_of(r * stride, 8)
                window = jnp.concatenate(
                    [
                        comp_v[pl.ds(base, 2 * pulses), :].astype(jnp.bfloat16),
                        comp_v[pl.ds(base + stride, 2 * pulses), :].astype(jnp.bfloat16),
                    ],
                    axis=1,
                )
                value = dot(window, band).astype(jnp.bfloat16)
                at = pl.multiple_of(t * LANES, LANES)
                out_ref[0, :, pl.ds(at, LANES)] = value[:pulses]
                out_ref[1, :, pl.ds(at, LANES)] = value[pulses:]
                return carry

            lax.fori_loop(0, tiles, migrate_step, 0, unroll=math.gcd(tiles, 16) if tiles > 16 else tiles)
            group_base += tiles


def range_call(z, raw, phase, starts, weights, tables, first_pulse, pulses, bin_count, group_tiles):
    heights = raw.shape[-1] // LANES
    pair = 4
    stride = 2 * pulses + 8
    plan = (first_pulse, pulses, bin_count, tuple(group_tiles), pair)
    vmem = pl.BlockSpec(memory_space=pltpu.VMEM)
    return pl.pallas_call(
        functools.partial(range_kernel, plan),
        out_shape=[
            jax.ShapeDtypeStruct((2, pulses, tiles * LANES), jnp.bfloat16)
            for tiles in group_tiles
            for _ in range(bin_count)
        ],
        in_specs=[pl.BlockSpec(memory_space=pltpu.SMEM), pl.BlockSpec(memory_space=pl.ANY)] + [vmem] * (3 + len(tables)),
        out_specs=[vmem] * (bin_count * len(group_tiles)),
        scratch_shapes=[
            pltpu.VMEM((2, pulses, raw.shape[-1]), jnp.bfloat16),
            pltpu.VMEM((2 * heights * SLAB, LANES), jnp.float32),
            pltpu.VMEM(((heights + 1) * stride, LANES), jnp.float32),
            pltpu.VMEM((2, heights, LANES), jnp.float32),
            pltpu.SemaphoreType.DMA((pulses // SLAB,)),
        ],
        compiler_params=pltpu.CompilerParams(vmem_limit_bytes=VMEM_BYTES),
        cost_estimate=pl.CostEstimate(
            flops=COST, bytes_accessed=COST, transcendentals=0
        ),
        name="range_lines",
    )(z, raw, phase, starts, weights, *tables)


def range_tables(width):
    heights = width // LANES
    first = unit_roots(np.arange(heights), np.arange(heights), heights)
    second = unit_roots(np.arange(LANES), np.arange(LANES), LANES)
    twiddle = np.stack(unit_roots(np.arange(heights), np.arange(LANES), width)).astype(np.float32)
    return (
        twiddle,
        left_table(*first, -1.0),
        right_table(*second, -1.0),
        right_table(*second, 1.0, 1.0 / LANES),
        left_table(*first, 1.0, 1.0 / heights),
    )


def head_kernel(sources, masks, z_ref, *rest):
    in_refs, out_ref, sem = rest[:masks], rest[masks], rest[masks + 1]
    z = z_ref[0]
    for source in range(sources):
        wanted = lax.bitwise_xor(z, source)
        for mask in range(masks):

            @pl.when(wanted == mask)
            def _(mask=mask, source=source):
                pltpu.make_async_copy(in_refs[mask], out_ref.at[source], sem.at[source]).start()

    for source in range(sources):
        pltpu.make_async_copy(in_refs[0], out_ref.at[source], sem.at[source]).wait()


def pick_head(z, pieces, sources):
    shape = pieces[0].shape
    return pl.pallas_call(
        functools.partial(head_kernel, sources, len(pieces)),
        out_shape=jax.ShapeDtypeStruct((sources,) + shape, jnp.bfloat16),
        in_specs=[pl.BlockSpec(memory_space=pltpu.SMEM)] + [pl.BlockSpec(memory_space=pl.ANY)] * len(pieces),
        out_specs=pl.BlockSpec(memory_space=pltpu.VMEM),
        scratch_shapes=[pltpu.SemaphoreType.DMA((sources,))],
        compiler_params=pltpu.CompilerParams(vmem_limit_bytes=VMEM_BYTES),
        name="pick_head",
    )(z, *pieces)


def azimuth_kernel(plan, z_ref, length_ref, rate_ref, forward_hbm, inverse_hbm, *rest):
    parts, device_pulses, bin_count, lane_offset, width, tile, chained = plan
    count = len(parts) * (bin_count + 1)
    piece_refs = rest[:count]
    rest = rest[count + (1 if chained else 0) :]
    image_ref, forward_ref, inverse_ref, aperture_v, spectrum_v, narrow_v, image_v, sems, table_sems, out_sem = rest
    z = z_ref[0]
    lines = image_ref.shape[2]
    length = aperture_v.shape[1]
    half = length // 2
    copies = []
    at = 0
    for start, pulses, from_lane in parts:
        lanes = pl.ds(from_lane, width)
        for mask in range(bin_count):
            source = lax.bitwise_xor(z, mask)
            row = pl.multiple_of(source * device_pulses + start, SLAB)
            copies.append(
                pltpu.make_async_copy(
                    piece_refs[at].at[:, :, lanes], aperture_v.at[:, pl.ds(row, pulses), :], sems.at[len(copies)]
                )
            )
            at += 1
        heads = piece_refs[at]
        at += 1
        for source in range(heads.shape[0]):
            row = lines + source * device_pulses + start
            copies.append(
                pltpu.make_async_copy(
                    heads.at[source, :, :, lanes], aperture_v.at[:, pl.ds(row, pulses), :], sems.at[len(copies)]
                )
            )
    tables = [
        pltpu.make_async_copy(forward_hbm, forward_ref, table_sems.at[0]),
        pltpu.make_async_copy(inverse_hbm, inverse_ref, table_sems.at[1]),
    ]
    for copy in copies + tables:
        copy.start()
    for copy in copies:
        copy.wait()

    def row_of(ref, lane):
        first = (lane_offset + lane) // LANES
        return jnp.concatenate([ref[pl.ds(first + i, 1), :] for i in range(tile // LANES)], axis=1)

    block = 64
    outs = []
    for lane in range(0, width, tile):
        lanes = pl.ds(lane, tile)
        reach = row_of(length_ref, lane)
        for row in range(lines, length, SLAB):
            pulse = lax.broadcasted_iota(jnp.int32, (SLAB, tile), 0) + (row - lines)
            inside = pulse < reach
            for comp in range(2):
                held = aperture_v[comp, pl.ds(row, SLAB), lanes].astype(jnp.float32)
                aperture_v[comp, pl.ds(row, SLAB), lanes] = jnp.where(inside, held, 0.0).astype(jnp.bfloat16)
        real, imag = aperture_v[0, :, lanes], aperture_v[1, :, lanes]
        pair = jnp.concatenate(
            [jnp.concatenate([real, imag], axis=0), jnp.concatenate([imag, -real], axis=0)], axis=1
        )
        if lane == 0:
            tables[0].wait()
        spectrum_v[...] = dot(forward_ref[...], pair)
        rate = row_of(rate_ref, lane)

        def filter_rows(cosine, sine, row, size):
            real = spectrum_v[pl.ds(row, size), :tile]
            imag = spectrum_v[pl.ds(row, size), tile:]
            turned_real = (real * cosine + imag * sine).astype(jnp.bfloat16)
            turned_imag = (imag * cosine - real * sine).astype(jnp.bfloat16)
            narrow_v[pl.ds(row, size), :tile] = turned_real
            narrow_v[pl.ds(row, size), tile:] = turned_imag
            narrow_v[pl.ds(length + row, size), :tile] = -turned_imag
            narrow_v[pl.ds(length + row, size), tile:] = turned_real

        def doppler_phase(doppler):
            return turn_pair(rate * (doppler * doppler * (0.5 / length)))

        for row in range(0, half, block):
            doppler = (lax.broadcasted_iota(jnp.int32, (block, tile), 0) + row).astype(jnp.float32)
            cosine, sine = doppler_phase(doppler)
            filter_rows(cosine, sine, row, block)
            if row == 0:
                top = doppler[:SLAB]
                top_cos, top_sin = doppler_phase(jnp.where(top == 0.0, float(half), top))
                filter_rows(top_cos, top_sin, half, SLAB)
                filter_rows(cosine[SLAB:], sine[SLAB:], half + SLAB, block - SLAB)
            else:
                filter_rows(cosine, sine, half + row, block)

        if lane == 0:
            tables[1].wait()
        image = dot(inverse_ref[...], narrow_v[...]) * (1.0 / length)
        image_v[0, :, lanes] = image[:, :tile].astype(jnp.bfloat16)
        image_v[1, :, lanes] = image[:, tile:].astype(jnp.bfloat16)
        outs.append(
            pltpu.make_async_copy(
                image_v.at[:, :, lanes],
                image_ref.at[:, 0, :, pl.ds(lane_offset + lane, tile)],
                out_sem.at[lane // tile],
            )
        )
        outs[-1].start()
    for out in outs:
        out.wait()


def azimuth_call(z, lengths, rates, tables, pieces, parts, device_pulses, bin_count, lane_offset, width, image_shape, image):
    vmem = pl.BlockSpec(memory_space=pltpu.VMEM)
    lines = image_shape[2]
    length = lines + OVLMAX
    tile = next(t * LANES for t in (4, 3, 2, 1) if width % (t * LANES) == 0)
    chained = image is not None
    plan = (tuple(parts), device_pulses, bin_count, lane_offset, width, tile, chained)
    sources = pieces[bin_count].shape[0]
    operands = [z, lengths, rates, *tables, *pieces] + ([image] if chained else [])
    any_spec = pl.BlockSpec(memory_space=pl.ANY)
    return pl.pallas_call(
        functools.partial(azimuth_kernel, plan),
        out_shape=jax.ShapeDtypeStruct(image_shape, jnp.bfloat16),
        in_specs=[pl.BlockSpec(memory_space=pltpu.SMEM)] + [vmem] * 2 + [any_spec] * (len(operands) - 3),
        out_specs=any_spec,
        scratch_shapes=[
            pltpu.VMEM(tables[0].shape, jnp.bfloat16),
            pltpu.VMEM(tables[1].shape, jnp.bfloat16),
            pltpu.VMEM((2, length, width), jnp.bfloat16),
            pltpu.VMEM((length, 2 * tile), jnp.float32),
            pltpu.VMEM((2 * length, 2 * tile), jnp.bfloat16),
            pltpu.VMEM((2, lines, width), jnp.bfloat16),
            pltpu.SemaphoreType.DMA((len(parts) * (bin_count + sources),)),
            pltpu.SemaphoreType.DMA((2,)),
            pltpu.SemaphoreType.DMA((width // tile,)),
        ],
        input_output_aliases={len(operands) - 1: 0} if chained else {},
        compiler_params=pltpu.CompilerParams(vmem_limit_bytes=VMEM_BYTES),
        cost_estimate=pl.CostEstimate(
            flops=COST,
            bytes_accessed=COST,
            transcendentals=0,
        ),
        name="azimuth_bins",
    )(*operands)


def azimuth_tables(lines):
    length = lines + OVLMAX
    half = length // 2
    order = np.concatenate([np.arange(half), [half], length - np.arange(1, half)])
    forward = np.concatenate(unit_roots(order, np.arange(length), length), axis=1)
    inverse = np.concatenate(unit_roots(np.arange(lines), order, length), axis=1)
    return forward.astype(ml_dtypes.bfloat16), inverse.astype(ml_dtypes.bfloat16)


def exchanged(value, mask):
    count = lax.axis_size("bins")
    return lax.ppermute(value, "bins", [(s, s ^ mask) for s in range(count)]) if mask else value


def passed_back(value):
    count = lax.axis_size("az")
    return lax.ppermute(value, "az", [(s, s - 1) for s in range(1, count)])


def split_tiles(tiles):
    ends = sorted({max(1, round(tiles * f)) for f in ENDS} | {tiles})
    return [b - a for a, b in zip([0] + ends[:-1], ends)]


def shards(raw_echoes, range_phase, band_start, band_weight, intersection_length, azimuth_rate):
    bin_count = lax.axis_size("bins")
    width = raw_echoes.shape[-1]
    heights = width // LANES
    device_pulses = raw_echoes.shape[2]
    lines = device_pulses * bin_count
    device_bins = width // bin_count
    device_tiles = device_bins // LANES
    z = lax.axis_index("bins").astype(jnp.int32).reshape(1)
    phase = range_phase.reshape(LANES, heights)
    starts = band_start.reshape(heights, LANES)
    tables = [jnp.asarray(t) for t in range_tables(width)]
    sources = max(1, OVLMAX // device_pulses)
    first = max(SLAB, device_pulses // FIRST // SLAB * SLAB)
    shares = split_tiles(device_tiles)

    def line_call(turn, at, pulses, tiles):
        return range_call(turn, raw_echoes, phase, starts, band_weight, tables, at, pulses, bin_count, tiles)

    early = line_call(z, 0, first, [device_tiles])
    late_z, early = lax.optimization_barrier((z, early))
    early = [exchanged(v, m) for m, v in enumerate(early)]
    late = line_call(late_z, first, device_pulses - first, shares)
    early, late = lax.optimization_barrier((early, late))
    early_head = passed_back(pick_head(z, early, sources))
    late = [
        [exchanged(v, m) for m, v in enumerate(late[g * bin_count : (g + 1) * bin_count])] for g in range(len(shares))
    ]
    az_tables = [jnp.asarray(t) for t in azimuth_tables(lines)]
    image_shape = (2, 1, lines, device_bins)
    lengths = intersection_length.reshape(device_tiles, LANES)
    rates = azimuth_rate.reshape(device_tiles, LANES)
    offset = 0
    image = None
    head = passed_back(pick_head(z, late[0], sources))
    for g, share in enumerate(shares):
        pieces, next_head, turn = late[g], None, z
        if g + 1 < len(shares):
            if image is not None:
                turn, image = lax.optimization_barrier((z, image))
            ahead = pick_head(turn, late[g + 1], sources)
            next_head = passed_back(ahead)
            turn, _ = lax.optimization_barrier((z, late[g + 1][bin_count // 2]))
        image = azimuth_call(
            turn,
            lengths,
            rates,
            az_tables,
            [*early, early_head, *pieces, head],
            [(0, first, offset), (first, device_pulses - first, 0)],
            device_pulses,
            bin_count,
            offset,
            share * LANES,
            image_shape,
            image,
        )
        head = next_head
        offset += share * LANES
    return image


def solution(mesh):
    in_specs = (P(None, ("scene", "az"), "bins", None), P(), P(), P(), P("bins"), P("bins"))
    out_specs = P(None, ("scene", "az"), None, "bins")
    return jax.shard_map(shards, mesh=mesh, in_specs=in_specs, out_specs=out_specs, check_vma=False)
```
